32 devices in a mesh: dp: 8 (over z, x), tensor: 4 (over y, core).
Axes of the slice: x: 2, y: 2, z: 4, core: 2. Of those that a mesh axis runs over, the one named last changes fastest.
Arguments:
- activations: bfloat16 [2048, 4096], P('dp'), may hold values from -6 to 6
- grad_output: bfloat16 [2048, 14336], P('dp', 'tensor'), may hold values from -6 to 6
- weight: bfloat16 [4096, 14336], P('dp', 'tensor'), may hold values from -0.09375 to 0.09375
- start_basis: float32 [14336, 64], P('tensor'), may hold values from -6 to 6
Outputs:
- input_grad: bfloat16 [2048, 4096], P('dp', 'tensor')
- right_basis: float32 [14336, 64], P('tensor')
- new_weight: float32 [4096, 14336], P('dp', 'tensor')
The draws below stay inside these ranges and needn't reach their ends.
All inputs are finite; a program needn't handle non-finite values.
Results may differ from the reference program's by a relative error of at most 0.018.
Values may be sent and summed in bfloat16 or wider, within the bound.
A program may use at most 128 MiB of HBM per device.

```python
import jax
import jax.numpy as jnp
from jax import lax

D = 4096
FF = 14336
RANK = 64
TOKENS = 2048
N_TENSOR = 4


def steps_of(own_key, extent, split, low, high):
    factor_of, own = 1.0, jax.random.fold_in(own_key, 6)
    for position, parts in split:
        draws = jnp.exp(jax.random.uniform(jax.random.fold_in(own, position), (parts,), jnp.float32, low / len(split), high / len(split)))
        factor_of = factor_of * jnp.repeat(draws, extent[position] // parts).reshape([-1 if axis == position else 1 for axis in range(len(extent))])
    return factor_of


def noise(stream_key, dims, spread, limit, shards=(), held_as=jnp.bfloat16):
    level = steps_of(stream_key, dims, shards, -0.22, 0.18) if shards else 1.0
    entries = jax.random.normal(stream_key, dims, jnp.float32) * spread * level
    return jnp.minimum(jnp.maximum(entries, -limit), limit).astype(held_as)


def setup_inputs(seed: int = 0) -> dict:
    streams_of = jax.random.split(jax.random.key(seed), 5)
    activations = noise(streams_of[0], (TOKENS, D), 1.0, 6.0, ((0, 8),))
    grad_output = noise(streams_of[1], (TOKENS, FF), 1.0, 6.0, ((0, 8), (1, 4)))
    weight = noise(streams_of[2], (D, FF), D ** -0.5, 0.09375, ((0, 8), (1, 4)))
    start_basis = noise(streams_of[3], (FF, RANK), 1.0, 6.0, ((0, 4),), jnp.float32)
    return {"activations": activations, "grad_output": grad_output, "weight": weight, "start_basis": start_basis}


learn_rate = 0.001

def reference(activations, grad_output, weight, start_basis):
    block_width = FF // N_TENSOR
    grad_blocks = grad_output.reshape(TOKENS, N_TENSOR, block_width).transpose(1, 0, 2)
    weight_blocks = weight.reshape(D, N_TENSOR, block_width).transpose(1, 0, 2)

    def add_block(total, pair):
        grad_piece, weight_piece = pair
        partial_sum = lax.dot_general(grad_piece.astype(jnp.float32), weight_piece.astype(jnp.float32), (((1,), (1,)), ((), ())), preferred_element_type=jnp.float32)
        return (total + partial_sum.astype(jnp.bfloat16).astype(jnp.float32), None)
    summed, _ = lax.scan(add_block, jnp.zeros((TOKENS, D), jnp.float32), (grad_blocks, weight_blocks))
    input_grad = summed.astype(jnp.bfloat16)
    gradient = lax.dot_general(activations.astype(jnp.float32), grad_output.astype(jnp.float32), (((0,), (0,)), ((), ())), preferred_element_type=jnp.float32)
    left = jnp.dot(gradient, start_basis, precision=lax.Precision.HIGHEST)
    gram_matrix = jnp.dot(left.T, left, precision=lax.Precision.HIGHEST)
    lower = jnp.linalg.cholesky(gram_matrix)
    left_basis = jax.scipy.linalg.solve_triangular(lower, left.T, lower=True).T
    right = jnp.dot(gradient.T, left_basis, precision=lax.Precision.HIGHEST)
    right_basis = right / jnp.sqrt(jnp.float32(TOKENS))
    update = jnp.dot(left_basis, right.T, precision=lax.Precision.HIGHEST)
    new_weight = weight.astype(jnp.float32) - learn_rate * update
    return (input_grad, right_basis, new_weight)
```

```python
import jax
import jax.numpy as jnp
from jax import lax
from jax.sharding import PartitionSpec as P

learn_rate = 0.001


def orthonormal_basis(left):
    gram_matrix = jnp.dot(left.T, left, precision=lax.Precision.HIGHEST)
    lower = jnp.linalg.cholesky(gram_matrix)
    return lower


def split_parts(values):
    upper_part = values.astype(jnp.bfloat16)
    lower_part = (values - upper_part.astype(jnp.float32)).astype(jnp.bfloat16)
    return (upper_part, lower_part)


def thin_product(wide, thin_values, dims):
    upper_part, lower_part = split_parts(thin_values)
    first = lax.dot_general(wide, upper_part, dims, preferred_element_type=jnp.float32)
    second = lax.dot_general(wide, lower_part, dims, preferred_element_type=jnp.float32)
    return first + second


def body(activations, grad_output, weight, start_basis):
    count = lax.axis_size("dp")
    groups = count // 2
    index = lax.axis_index("dp")
    group = index // 2
    swap = [(i, i + 1 - 2 * (i % 2)) for i in range(count)]
    ahead = [(i, (i + 2) % count) for i in range(count)]
    behind = [(i, (i - 2) % count) for i in range(count)]
    other = lax.ppermute(weight, "dp", swap)
    low = index % 2 == 0
    weight_pair = jnp.concatenate(
        [jnp.where(low, weight, other), jnp.where(low, other, weight)], axis=0
    )
    tokens = grad_output.shape[0]
    half = tokens // 2
    upper, under = grad_output[:half], grad_output[half:]
    columns = weight_pair.shape[0]
    partial = jnp.zeros((groups, tokens, columns), jnp.bfloat16)
    for step in range(groups):
        if step + 1 < groups:
            next_upper = lax.ppermute(upper, "dp", ahead)
            next_under = lax.ppermute(under, "dp", behind)
        for piece, source, row in (
            (upper, (group - step + groups) % groups, 0),
            (under, (group + step) % groups, half),
        ):
            product = lax.dot_general(
                piece, weight_pair, (((1,), (1,)), ((), ())), preferred_element_type=jnp.float32
            ).astype(jnp.bfloat16)
            partial = lax.dynamic_update_slice(partial, product[None], (source, row, 0))
        if step + 1 < groups:
            upper, under = next_upper, next_under
    summed = lax.psum_scatter(partial, "tensor", scatter_dimension=1, tiled=True)
    along = [[2 * g + b for g in range(groups)] for b in range(2)]
    summed = lax.all_to_all(summed, "dp", 0, 0, axis_index_groups=along, tiled=True)
    rows = summed.shape[1]
    summed = summed.transpose(1, 0, 2).reshape(rows, groups * columns)
    input_grad = lax.all_to_all(summed, "tensor", 1, 0, tiled=True)
    plain_dims = (((1,), (0,)), ((), ()))
    token_dims = (((0,), (0,)), ((), ()))
    thin_rows = thin_product(grad_output, start_basis, plain_dims)
    left_part = thin_product(activations, thin_rows, token_dims)
    left = lax.psum(left_part, ("dp", "tensor"))
    lower = orthonormal_basis(left)
    left_basis = jax.scipy.linalg.solve_triangular(lower, left.T, lower=True).T
    token_proj = thin_product(activations, left_basis, plain_dims)
    right_part = thin_product(grad_output, token_proj, token_dims)
    right = lax.psum(right_part.astype(jnp.bfloat16), "dp").astype(jnp.float32)
    token_total = activations.shape[0] * lax.axis_size("dp")
    right_basis = right / jnp.sqrt(jnp.float32(token_total))
    row_count = weight.shape[0]
    offset = lax.axis_index("dp") * row_count
    basis_mine = lax.dynamic_slice_in_dim(left_basis, offset, row_count, 0)
    update = jnp.dot(basis_mine, right.T, precision=lax.Precision.HIGHEST)
    new_weight = weight.astype(jnp.float32) - learn_rate * update
    return (input_grad, right_basis, new_weight)


def solution(mesh):
    return jax.shard_map(
        body,
        mesh=mesh,
        in_specs=(P("dp", None), P("dp", "tensor"), P("dp", "tensor"), P("tensor", None)),
        out_specs=(P("dp", "tensor"), P("tensor", None), P("dp", "tensor")),
        check_vma=False,
    )
```

```python
import jax
import jax.numpy as jnp
from jax import lax
from jax.sharding import PartitionSpec as P

learn_rate = 0.001
highest = lax.Precision.HIGHEST
tie = lax.optimization_barrier


def split_parts(values):
    upper_part = values.astype(jnp.bfloat16)
    lower_part = (values - upper_part.astype(jnp.float32)).astype(jnp.bfloat16)
    return (upper_part, lower_part)


def thin_product(thin_values, wide, wide_dim):
    rank = thin_values.shape[0]
    both = lax.dot_general(
        jnp.concatenate(split_parts(thin_values), axis=0),
        wide,
        (((1,), (wide_dim,)), ((), ())),
        preferred_element_type=jnp.float32,
    )
    return both[:rank] + both[rank:]


def spread(values, axis, groups=None):
    count = lax.axis_size(axis) if groups is None else len(groups[0])
    copies = jnp.broadcast_to(values[None], (count,) + values.shape)
    return lax.all_to_all(copies, axis, 0, 0, axis_index_groups=groups, tiled=True)


def body(activations, grad_output, weight, start_basis):
    count, width = lax.axis_size("dp"), lax.axis_size("tensor")
    index, lane = lax.axis_index("dp"), lax.axis_index("tensor")
    groups = count // 2
    group = index // 2
    tokens, depth = activations.shape
    row_count = weight.shape[0]
    half = tokens // 2
    swap = [(i, i + 1 - 2 * (i % 2)) for i in range(count)]
    ahead = [(i, (i + 2) % count) for i in range(count)]
    behind = [(i, (i - 2) % count) for i in range(count)]
    along = [[2 * g + b for g in range(groups)] for b in range(2)]
    share = depth // width
    activations_mine = lax.dynamic_slice_in_dim(activations, lane * share, share, 1)

    def left_stage():
        thin_rows = spread(thin_product(start_basis.T, grad_output, 1), "tensor").sum(0)
        left_part = thin_product(thin_rows, activations_mine, 0)
        rank = left_part.shape[0]
        pieces = left_part.reshape(rank, count, share // count).transpose(1, 0, 2)
        left_piece = lax.all_to_all(pieces, "dp", 0, 0, tiled=True).sum(0)
        return spread(left_piece, "dp").transpose(1, 0, 2).reshape(rank, share)

    def basis_stage(left):
        rank = left.shape[0]
        raw_proj = thin_product(left, activations_mine, 1)
        gram_part = lax.dot_general(left, left, (((1,), (1,)), ((), ())), precision=highest)
        both = spread(jnp.concatenate([raw_proj, gram_part], axis=1), "tensor").sum(0)
        lower = jnp.linalg.cholesky(both[:, tokens:])
        inverse = jax.scipy.linalg.solve_triangular(lower, jnp.eye(rank, dtype=jnp.float32), lower=True)
        token_proj = jnp.dot(inverse, both[:, :tokens], precision=highest)
        per_share = share // row_count
        rows = lax.dynamic_slice_in_dim(left, (index % per_share) * row_count, row_count, 1)
        rows = lax.dynamic_index_in_dim(spread(rows, "tensor"), index // per_share, 0, False)
        basis_mine = jnp.dot(inverse, rows, precision=highest)
        return spread(token_proj, "dp", along), basis_mine

    other = lax.ppermute(weight, "dp", swap)
    low = index % 2 == 0
    weight_pair = jnp.concatenate(
        [jnp.where(low, weight, other), jnp.where(low, other, weight)], axis=0
    )
    columns = weight_pair.shape[0]
    upper, under = grad_output[:half], grad_output[half:]
    gathered = jnp.zeros((groups, 2, half, grad_output.shape[1]), jnp.bfloat16)
    summed = jnp.zeros((groups, 2, half // width, columns), jnp.bfloat16)
    for step in range(groups):
        if step + 1 < groups:
            next_upper = lax.ppermute(upper, "dp", ahead)
            next_under = lax.ppermute(under, "dp", behind)
        sources = ((group - step + groups) % groups, (group + step) % groups)
        products = []
        for place, (piece, source) in enumerate(zip((upper, under), sources)):
            gathered = lax.dynamic_update_slice(gathered, piece[None, None], (source, place, 0, 0))
            product = lax.dot_general(
                piece, weight_pair, (((1,), (1,)), ((), ())), preferred_element_type=jnp.float32
            )
            products.append(product.astype(jnp.bfloat16).reshape(width, half // width, columns))
        parts = lax.all_to_all(jnp.stack(products, axis=1), "tensor", 0, 0, tiled=True)
        total = parts.astype(jnp.float32).sum(0).astype(jnp.bfloat16)
        for place, source in enumerate(sources):
            summed = lax.dynamic_update_slice(summed, total[place][None, None], (source, place, 0, 0))
        if step == 0:
            left = left_stage()
            next_upper, next_under, left = tie((next_upper, next_under, left))
        if step == 1:
            token_proj, basis_mine = basis_stage(left)
            next_upper, next_under, token_proj = tie((next_upper, next_under, token_proj))
        if step + 1 < groups:
            upper, under = next_upper, next_under

    rank = start_basis.shape[1]
    right_part = thin_product(
        token_proj.transpose(1, 0, 2).reshape(rank, groups * tokens),
        gathered.reshape(groups * tokens, -1),
        0,
    ).astype(jnp.bfloat16)
    right_other = lax.ppermute(right_part, "dp", swap)
    right = right_part.astype(jnp.float32) + right_other.astype(jnp.float32)
    right_basis = (right / jnp.sqrt(jnp.float32(tokens * count))).T

    moved = lax.all_to_all(summed, "dp", 0, 0, axis_index_groups=along, tiled=True)
    moved = moved.reshape(groups, 2 * (half // width), columns).transpose(1, 0, 2)
    moved = moved.reshape(2, half // width, width, share).transpose(2, 0, 1, 3)
    moved = lax.all_to_all(moved, "tensor", 0, 0, tiled=True)
    input_grad = moved.transpose(1, 0, 2, 3).reshape(tokens, share)

    basis_upper, basis_lower = split_parts(basis_mine)
    update = lax.dot_general(
        jnp.concatenate([basis_upper, basis_upper, basis_lower, basis_lower], axis=0),
        jnp.concatenate([right_part, right_other, right_part, right_other], axis=0),
        (((0,), (0,)), ((), ())),
        preferred_element_type=jnp.float32,
    )
    new_weight = weight.astype(jnp.float32) - learn_rate * update
    return (input_grad, right_basis, new_weight)


def solution(mesh):
    return jax.shard_map(
        body,
        mesh=mesh,
        in_specs=(P("dp", None), P("dp", "tensor"), P("dp", "tensor"), P("tensor", None)),
        out_specs=(P("dp", "tensor"), P("tensor", None), P("dp", "tensor")),
        check_vma=False,
    )
```

```python
import jax
import jax.numpy as jnp
from jax import lax
from jax.sharding import PartitionSpec as P

learn_rate = 0.001
highest = lax.Precision.HIGHEST
tie = lax.optimization_barrier


def split_parts(values):
    upper_part = values.astype(jnp.bfloat16)
    lower_part = (values - upper_part.astype(jnp.float32)).astype(jnp.bfloat16)
    return (upper_part, lower_part)


def thin_product(thin_values, wide, wide_dim):
    rank = thin_values.shape[0]
    both = lax.dot_general(
        jnp.concatenate(split_parts(thin_values), axis=0),
        wide,
        (((1,), (wide_dim,)), ((), ())),
        preferred_element_type=jnp.float32,
    )
    return both[:rank] + both[rank:]


def spread(values, axis, groups=None):
    count = lax.axis_size(axis) if groups is None else len(groups[0])
    copies = jnp.broadcast_to(values[None], (count,) + values.shape)
    return lax.all_to_all(copies, axis, 0, 0, axis_index_groups=groups, tiled=True)


def body(activations, grad_output, weight, start_basis):
    count, width = lax.axis_size("dp"), lax.axis_size("tensor")
    index, lane = lax.axis_index("dp"), lax.axis_index("tensor")
    groups = count // 2
    group = index // 2
    tokens, depth = activations.shape
    row_count = weight.shape[0]
    half = tokens // 2
    swap = [(i, i + 1 - 2 * (i % 2)) for i in range(count)]
    ahead = [(i, (i + 2) % count) for i in range(count)]
    behind = [(i, (i - 2) % count) for i in range(count)]
    along = [[2 * g + b for g in range(groups)] for b in range(2)]
    share = depth // width
    activations_mine = lax.dynamic_slice_in_dim(activations, lane * share, share, 1)

    def left_stage():
        thin_rows = spread(thin_product(start_basis.T, grad_output, 1), "tensor").sum(0)
        left_part = thin_product(thin_rows, activations_mine, 0)
        rank = left_part.shape[0]
        pieces = left_part.reshape(rank, count, share // count).transpose(1, 0, 2)
        left_piece = lax.all_to_all(pieces, "dp", 0, 0, tiled=True).sum(0)
        return spread(left_piece, "dp").transpose(1, 0, 2).reshape(rank, share)

    def basis_stage(left):
        rank = left.shape[0]
        raw_proj = thin_product(left, activations_mine, 1)
        gram_part = lax.dot_general(left, left, (((1,), (1,)), ((), ())), precision=highest)
        both = spread(jnp.concatenate([raw_proj, gram_part], axis=1), "tensor").sum(0)
        lower = jnp.linalg.cholesky(both[:, tokens:])
        inverse = jax.scipy.linalg.solve_triangular(lower, jnp.eye(rank, dtype=jnp.float32), lower=True)
        token_proj = jnp.dot(inverse, both[:, :tokens], precision=highest)
        per_share = share // row_count
        rows = lax.dynamic_slice_in_dim(left, (index % per_share) * row_count, row_count, 1)
        rows = lax.dynamic_index_in_dim(spread(rows, "tensor"), index // per_share, 0, False)
        basis_mine = jnp.dot(inverse, rows, precision=highest)
        return token_proj, basis_mine

    left = left_stage()
    weight_sent, grad_sent, left = tie((weight, grad_output, left))
    other = lax.ppermute(weight_sent, "dp", swap)
    low = index % 2 == 0
    weight_pair = jnp.concatenate(
        [jnp.where(low, weight, other), jnp.where(low, other, weight)], axis=0
    )
    columns = weight_pair.shape[0]
    piece_rows = half // width
    upper, under = grad_sent[:half], grad_sent[half:]
    gathered = jnp.zeros((groups, 2, half, grad_output.shape[1]), jnp.bfloat16)
    returned = jnp.zeros((groups, 2, piece_rows, columns), jnp.bfloat16)

    def reduced(pieces):
        product = lax.dot_general(
            jnp.concatenate(pieces, axis=0), weight_pair, (((1,), (1,)), ((), ())),
            preferred_element_type=jnp.float32,
        ).astype(jnp.bfloat16)
        product = product.reshape(len(pieces), width, piece_rows, columns).transpose(1, 0, 2, 3)
        parts = lax.all_to_all(product, "tensor", 0, 0, tiled=True)
        return parts.astype(jnp.float32).sum(0).astype(jnp.bfloat16)

    def give_back(returned, total, step):
        for place, sign in enumerate((1, -1)):
            value = total[place]
            if step:
                back = [(i, (i - 2 * sign * step) % count) for i in range(count)]
                value = lax.ppermute(value, "dp", back)
            source = (group + sign * step + groups) % groups
            returned = lax.dynamic_update_slice(returned, value[None, None], (source, place, 0, 0))
        return returned

    pieces = []
    for step in range(groups):
        if step == groups - 1:
            total = reduced(pieces)
            for earlier in range(step):
                returned = give_back(returned, total[2 * earlier : 2 * earlier + 2], earlier)
            total = reduced([upper, under])
            returned = give_back(returned, total, step)
        sources = ((group - step + groups) % groups, (group + step) % groups)
        for place, (piece, source) in enumerate(zip((upper, under), sources)):
            gathered = lax.dynamic_update_slice(gathered, piece[None, None], (source, place, 0, 0))
            pieces.append(piece)
        if step + 1 < groups:
            if step == 1:
                upper, under, token_proj = tie((upper, under, token_proj))
            if step == groups - 2:
                upper, under, weight_pair = tie((upper, under, weight_pair))
            upper = lax.ppermute(upper, "dp", ahead)
            under = lax.ppermute(under, "dp", behind)
        if step == 0:
            token_proj, basis_mine = basis_stage(left)
    token_proj = spread(token_proj, "dp", along)

    rank = start_basis.shape[1]
    right_part = thin_product(
        token_proj.transpose(1, 0, 2).reshape(rank, groups * tokens),
        gathered.reshape(groups * tokens, -1),
        0,
    ).astype(jnp.bfloat16)
    right_other = lax.ppermute(right_part, "dp", swap)
    right = right_part.astype(jnp.float32) + right_other.astype(jnp.float32)
    right_basis = (right / jnp.sqrt(jnp.float32(tokens * count))).T

    moved = returned
    moved = moved.reshape(groups, 2 * (half // width), columns).transpose(1, 0, 2)
    moved = moved.reshape(2, half // width, width, share).transpose(2, 0, 1, 3)
    moved = lax.all_to_all(moved, "tensor", 0, 0, tiled=True)
    input_grad = moved.transpose(1, 0, 2, 3).reshape(tokens, share)

    basis_upper, basis_lower = split_parts(basis_mine)
    update = lax.dot_general(
        jnp.concatenate([basis_upper, basis_upper, basis_lower, basis_lower], axis=0),
        jnp.concatenate([right_part, right_other, right_part, right_other], axis=0),
        (((0,), (0,)), ((), ())),
        preferred_element_type=jnp.float32,
    )
    new_weight = weight.astype(jnp.float32) - learn_rate * update
    return (input_grad, right_basis, new_weight)


def solution(mesh):
    return jax.shard_map(
        body,
        mesh=mesh,
        in_specs=(P("dp", None), P("dp", "tensor"), P("dp", "tensor"), P("tensor", None)),
        out_specs=(P("dp", "tensor"), P("tensor", None), P("dp", "tensor")),
        check_vma=False,
    )
```

```python
import jax
import jax.numpy as jnp
from jax import lax
from jax.sharding import PartitionSpec as P

learn_rate = 0.001
highest = lax.Precision.HIGHEST
tie = lax.optimization_barrier


def split_parts(values):
    upper_part = values.astype(jnp.bfloat16)
    lower_part = (values - upper_part.astype(jnp.float32)).astype(jnp.bfloat16)
    return (upper_part, lower_part)


def thin_product(thin_values, wide, wide_dim):
    rank = thin_values.shape[0]
    both = lax.dot_general(
        jnp.concatenate(split_parts(thin_values), axis=0),
        wide,
        (((1,), (wide_dim,)), ((), ())),
        preferred_element_type=jnp.float32,
    )
    return both[:rank] + both[rank:]


def spread(values, axis, groups=None):
    count = lax.axis_size(axis) if groups is None else len(groups[0])
    copies = jnp.broadcast_to(values[None], (count,) + values.shape)
    return lax.all_to_all(copies, axis, 0, 0, axis_index_groups=groups, tiled=True)


def body(activations, grad_output, weight, start_basis):
    count, width = lax.axis_size("dp"), lax.axis_size("tensor")
    index, lane = lax.axis_index("dp"), lax.axis_index("tensor")
    groups = count // 2
    group = index // 2
    tokens, depth = activations.shape
    row_count = weight.shape[0]
    half = tokens // 2
    swap = [(i, i + 1 - 2 * (i % 2)) for i in range(count)]
    ahead = [(i, (i + 2) % count) for i in range(count)]
    behind = [(i, (i - 2) % count) for i in range(count)]
    along = [[2 * g + b for g in range(groups)] for b in range(2)]
    share = depth // width
    activations_mine = lax.dynamic_slice_in_dim(activations, lane * share, share, 1)

    def left_stage():
        thin_rows = spread(thin_product(start_basis.T, grad_output, 1), "tensor").sum(0)
        left_part = thin_product(thin_rows, activations_mine, 0)
        rank = left_part.shape[0]
        pieces = left_part.reshape(rank, count, share // count).transpose(1, 0, 2)
        left_piece = lax.all_to_all(pieces, "dp", 0, 0, tiled=True).sum(0)
        return spread(left_piece, "dp").transpose(1, 0, 2).reshape(rank, share)

    def basis_stage(left):
        rank = left.shape[0]
        raw_proj = thin_product(left, activations_mine, 1)
        gram_part = lax.dot_general(left, left, (((1,), (1,)), ((), ())), precision=highest)
        both = spread(jnp.concatenate([raw_proj, gram_part], axis=1), "tensor").sum(0)
        lower = jnp.linalg.cholesky(both[:, tokens:])
        inverse = jax.scipy.linalg.solve_triangular(lower, jnp.eye(rank, dtype=jnp.float32), lower=True)
        token_proj = jnp.dot(inverse, both[:, :tokens], precision=highest)
        per_share = share // row_count
        rows = lax.dynamic_slice_in_dim(left, (index % per_share) * row_count, row_count, 1)
        rows = lax.dynamic_index_in_dim(spread(rows, "tensor"), index // per_share, 0, False)
        basis_mine = jnp.dot(inverse, rows, precision=highest)
        return token_proj, basis_mine

    cut = row_count // 2
    others = [lax.ppermute(weight[:cut], "dp", swap)]
    low = index % 2 == 0
    columns = 2 * row_count
    piece_rows = half // width
    upper, under = grad_output[:half], grad_output[half:]
    gathered = jnp.zeros((groups, 2, half, grad_output.shape[1]), jnp.bfloat16)
    returned = jnp.zeros((groups, 2, piece_rows, columns), jnp.bfloat16)

    def reduced(pieces):
        rows = jnp.concatenate(pieces, axis=0)
        mine, *rest = (
            lax.dot_general(
                rows, part, (((1,), (1,)), ((), ())), preferred_element_type=jnp.float32
            ).astype(jnp.bfloat16)
            for part in (weight, *others)
        )
        rest = jnp.concatenate(rest, axis=1)
        product = jnp.concatenate(
            [jnp.where(low, mine, rest), jnp.where(low, rest, mine)], axis=1
        )
        product = product.reshape(len(pieces), width, piece_rows, columns).transpose(1, 0, 2, 3)
        parts = lax.all_to_all(product, "tensor", 0, 0, tiled=True)
        return parts.astype(jnp.float32).sum(0).astype(jnp.bfloat16)

    def give_back(returned, total, step):
        for place, sign in enumerate((1, -1)):
            value = total[place]
            if step:
                back = [(i, (i - 2 * sign * step) % count) for i in range(count)]
                value = lax.ppermute(value, "dp", back)
            source = (group + sign * step + groups) % groups
            returned = lax.dynamic_update_slice(returned, value[None, None], (source, place, 0, 0))
        return returned

    pieces = []
    for step in range(groups):
        if step == groups - 1:
            total = reduced(pieces)
            for earlier in range(step):
                returned = give_back(returned, total[2 * earlier : 2 * earlier + 2], earlier)
            total = reduced([upper, under])
            returned = give_back(returned, total, step)
        sources = ((group - step + groups) % groups, (group + step) % groups)
        for place, (piece, source) in enumerate(zip((upper, under), sources)):
            gathered = lax.dynamic_update_slice(gathered, piece[None, None], (source, place, 0, 0))
            pieces.append(piece)
        if step + 1 < groups:
            if step == 1:
                left = left_stage()
                weight_sent, upper, under, left = tie((weight[cut:], upper, under, left))
                others.append(lax.ppermute(weight_sent, "dp", swap))
            if step == groups - 2:
                upper, under, others[1], token_proj = tie((upper, under, others[1], token_proj))
            upper = lax.ppermute(upper, "dp", ahead)
            under = lax.ppermute(under, "dp", behind)
            if step == 1:
                token_proj, basis_mine = basis_stage(left)
    token_proj = spread(token_proj, "dp", along)

    rank = start_basis.shape[1]
    right_part = thin_product(
        token_proj.transpose(1, 0, 2).reshape(rank, groups * tokens),
        gathered.reshape(groups * tokens, -1),
        0,
    ).astype(jnp.bfloat16)
    right_other = lax.ppermute(right_part, "dp", swap)
    right = right_part.astype(jnp.float32) + right_other.astype(jnp.float32)
    right_basis = (right / jnp.sqrt(jnp.float32(tokens * count))).T

    moved = returned
    moved = moved.reshape(groups, 2 * (half // width), columns).transpose(1, 0, 2)
    moved = moved.reshape(2, half // width, width, share).transpose(2, 0, 1, 3)
    moved = lax.all_to_all(moved, "tensor", 0, 0, tiled=True)
    input_grad = moved.transpose(1, 0, 2, 3).reshape(tokens, share)

    basis_upper, basis_lower = split_parts(basis_mine)
    update = lax.dot_general(
        jnp.concatenate([basis_upper, basis_upper, basis_lower, basis_lower], axis=0),
        jnp.concatenate([right_part, right_other, right_part, right_other], axis=0),
        (((0,), (0,)), ((), ())),
        preferred_element_type=jnp.float32,
    )
    new_weight = weight.astype(jnp.float32) - learn_rate * update
    return (input_grad, right_basis, new_weight)


def solution(mesh):
    return jax.shard_map(
        body,
        mesh=mesh,
        in_specs=(P("dp", None), P("dp", "tensor"), P("dp", "tensor"), P("tensor", None)),
        out_specs=(P("dp", "tensor"), P("tensor", None), P("dp", "tensor")),
        check_vma=False,
    )
```

```python
import jax
import jax.numpy as jnp
from jax import lax
from jax.sharding import PartitionSpec as P

learn_rate = 0.001
highest = lax.Precision.HIGHEST
tie = lax.optimization_barrier


def split_parts(values):
    upper_part = values.astype(jnp.bfloat16)
    lower_part = (values - upper_part.astype(jnp.float32)).astype(jnp.bfloat16)
    return (upper_part, lower_part)


def thin_product(thin_values, wide, wide_dim):
    rank = thin_values.shape[0]
    both = lax.dot_general(
        jnp.concatenate(split_parts(thin_values), axis=0),
        wide,
        (((1,), (wide_dim,)), ((), ())),
        preferred_element_type=jnp.float32,
    )
    return both[:rank] + both[rank:]


def spread(values, axis, groups=None):
    count = lax.axis_size(axis) if groups is None else len(groups[0])
    copies = jnp.broadcast_to(values[None], (count,) + values.shape)
    return lax.all_to_all(copies, axis, 0, 0, axis_index_groups=groups, tiled=True)


def body(activations, grad_output, weight, start_basis):
    count, width = lax.axis_size("dp"), lax.axis_size("tensor")
    index, lane = lax.axis_index("dp"), lax.axis_index("tensor")
    groups = count // 2
    group = index // 2
    tokens, depth = activations.shape
    row_count = weight.shape[0]
    half = tokens // 2
    swap = [(i, i + 1 - 2 * (i % 2)) for i in range(count)]
    ahead = [(i, (i + 2) % count) for i in range(count)]
    behind = [(i, (i - 2) % count) for i in range(count)]
    along = [[2 * g + b for g in range(groups)] for b in range(2)]
    share = depth // width
    activations_mine = lax.dynamic_slice_in_dim(activations, lane * share, share, 1)

    def left_stage():
        thin_rows = spread(thin_product(start_basis.T, grad_output, 1), "tensor").sum(0)
        left_part = thin_product(thin_rows, activations_mine, 0)
        rank = left_part.shape[0]
        pieces = left_part.reshape(rank, count, share // count).transpose(1, 0, 2)
        left_piece = lax.all_to_all(pieces, "dp", 0, 0, tiled=True).sum(0)
        return spread(left_piece, "dp").transpose(1, 0, 2).reshape(rank, share)

    def basis_stage(left):
        rank = left.shape[0]
        raw_proj = thin_product(left, activations_mine, 1)
        gram_part = lax.dot_general(left, left, (((1,), (1,)), ((), ())), precision=highest)
        both = spread(jnp.concatenate([raw_proj, gram_part], axis=1), "tensor").sum(0)
        lower = jnp.linalg.cholesky(both[:, tokens:])
        inverse = jax.scipy.linalg.solve_triangular(lower, jnp.eye(rank, dtype=jnp.float32), lower=True)
        token_proj = jnp.dot(inverse, both[:, :tokens], precision=highest)
        per_share = share // row_count
        rows = lax.dynamic_slice_in_dim(left, (index % per_share) * row_count, row_count, 1)
        rows = lax.dynamic_index_in_dim(spread(rows, "tensor"), index // per_share, 0, False)
        basis_mine = jnp.dot(inverse, rows, precision=highest)
        return token_proj, basis_mine

    cut = row_count // 4
    own = weight
    others = [lax.ppermute(weight[:cut], "dp", swap)]
    low = index % 2 == 0
    columns = 2 * row_count
    piece_rows = half // width
    upper, under = grad_output[:half], grad_output[half:]
    gathered = jnp.zeros((groups, 2, half, grad_output.shape[1]), jnp.bfloat16)
    returned = jnp.zeros((groups, 2, piece_rows, columns), jnp.bfloat16)

    def reduced(pieces):
        rows = jnp.concatenate(pieces, axis=0)
        mine, *rest = (
            lax.dot_general(
                rows, part, (((1,), (1,)), ((), ())), preferred_element_type=jnp.float32
            ).astype(jnp.bfloat16)
            for part in (own, *others)
        )
        rest = jnp.concatenate(rest, axis=1)
        product = jnp.concatenate(
            [jnp.where(low, mine, rest), jnp.where(low, rest, mine)], axis=1
        )
        product = product.reshape(len(pieces), width, piece_rows, columns).transpose(1, 0, 2, 3)
        parts = lax.all_to_all(product, "tensor", 0, 0, tiled=True)
        return parts.astype(jnp.float32).sum(0).astype(jnp.bfloat16)

    def give_back(returned, total, step):
        for place, sign in enumerate((1, -1)):
            value = total[place]
            if step:
                back = [(i, (i - 2 * sign * step) % count) for i in range(count)]
                value = lax.ppermute(value, "dp", back)
            source = (group + sign * step + groups) % groups
            returned = lax.dynamic_update_slice(returned, value[None, None], (source, place, 0, 0))
        return returned

    pieces = []
    for step in range(groups):
        if step == groups - 1:
            total = reduced(pieces)
            for earlier in range(step):
                returned = give_back(returned, total[2 * earlier : 2 * earlier + 2], earlier)
            upper, under, returned = tie((upper, under, returned))
            total = reduced([upper, under])
            returned = give_back(returned, total, step)
        sources = ((group - step + groups) % groups, (group + step) % groups)
        for place, (piece, source) in enumerate(zip((upper, under), sources)):
            gathered = lax.dynamic_update_slice(gathered, piece[None, None], (source, place, 0, 0))
            pieces.append(piece)
        if step + 1 < groups:
            if step == 1:
                left = left_stage()
                weight_sent, upper, under, left = tie((weight[cut:], upper, under, left))
                others.append(lax.ppermute(weight_sent, "dp", swap))
            if step == groups - 2:
                upper, under, own, others[0], token_proj = tie(
                    (upper, under, own, others[0], token_proj)
                )
            upper = lax.ppermute(upper, "dp", ahead)
            under = lax.ppermute(under, "dp", behind)
            if step == 1:
                token_proj, basis_mine = basis_stage(left)
                token_proj = spread(token_proj, "dp", along)
    rank = start_basis.shape[1]
    right_part = thin_product(
        token_proj.transpose(1, 0, 2).reshape(rank, groups * tokens),
        gathered.reshape(groups * tokens, -1),
        0,
    ).astype(jnp.bfloat16)
    right_other = lax.ppermute(right_part, "dp", swap)
    right = right_part.astype(jnp.float32) + right_other.astype(jnp.float32)
    right_basis = (right / jnp.sqrt(jnp.float32(tokens * count))).T

    moved = returned
    moved = moved.reshape(groups, 2 * (half // width), columns).transpose(1, 0, 2)
    moved = moved.reshape(2, half // width, width, share).transpose(2, 0, 1, 3)
    moved = lax.all_to_all(moved, "tensor", 0, 0, tiled=True)
    input_grad = moved.transpose(1, 0, 2, 3).reshape(tokens, share)

    basis_upper, basis_lower = split_parts(basis_mine)
    update = lax.dot_general(
        jnp.concatenate([basis_upper, basis_upper, basis_lower, basis_lower], axis=0),
        jnp.concatenate([right_part, right_other, right_part, right_other], axis=0),
        (((0,), (0,)), ((), ())),
        preferred_element_type=jnp.float32,
    )
    new_weight = weight.astype(jnp.float32) - learn_rate * update
    return (input_grad, right_basis, new_weight)


def solution(mesh):
    return jax.shard_map(
        body,
        mesh=mesh,
        in_specs=(P("dp", None), P("dp", "tensor"), P("dp", "tensor"), P("tensor", None)),
        out_specs=(P("dp", "tensor"), P("tensor", None), P("dp", "tensor")),
        check_vma=False,
    )
```

```python
import jax
import jax.numpy as jnp
from jax import lax
from jax.sharding import PartitionSpec as P

learn_rate = 0.001
highest = lax.Precision.HIGHEST
tie = lax.optimization_barrier


def split_parts(values):
    upper_part = values.astype(jnp.bfloat16)
    lower_part = (values - upper_part.astype(jnp.float32)).astype(jnp.bfloat16)
    return (upper_part, lower_part)


def thin_product(thin_values, wide, wide_dim):
    rank = thin_values.shape[0]
    both = lax.dot_general(
        jnp.concatenate(split_parts(thin_values), axis=0),
        wide,
        (((1,), (wide_dim,)), ((), ())),
        preferred_element_type=jnp.float32,
    )
    return both[:rank] + both[rank:]


def spread(values, axis, groups=None):
    count = lax.axis_size(axis) if groups is None else len(groups[0])
    copies = jnp.broadcast_to(values[None], (count,) + values.shape)
    return lax.all_to_all(copies, axis, 0, 0, axis_index_groups=groups, tiled=True)


def body(activations, grad_output, weight, start_basis):
    count, width = lax.axis_size("dp"), lax.axis_size("tensor")
    index, lane = lax.axis_index("dp"), lax.axis_index("tensor")
    groups = count // 2
    group = index // 2
    tokens, depth = activations.shape
    row_count = weight.shape[0]
    half = tokens // 2
    swap = [(i, i + 1 - 2 * (i % 2)) for i in range(count)]
    ahead = [(i, (i + 2) % count) for i in range(count)]
    behind = [(i, (i - 2) % count) for i in range(count)]
    along = [[2 * g + b for g in range(groups)] for b in range(2)]
    share = depth // width
    activations_mine = lax.dynamic_slice_in_dim(activations, lane * share, share, 1)

    def left_stage():
        thin_rows = spread(thin_product(start_basis.T, grad_output, 1), "tensor").sum(0)
        left_part = thin_product(thin_rows, activations_mine, 0)
        rank = left_part.shape[0]
        pieces = left_part.reshape(rank, count, share // count).transpose(1, 0, 2)
        left_piece = lax.all_to_all(pieces, "dp", 0, 0, tiled=True).sum(0)
        return spread(left_piece, "dp").transpose(1, 0, 2).reshape(rank, share)

    def basis_stage(left):
        rank = left.shape[0]
        raw_proj = thin_product(left, activations_mine, 1)
        gram_part = lax.dot_general(left, left, (((1,), (1,)), ((), ())), precision=highest)
        both = spread(jnp.concatenate([raw_proj, gram_part], axis=1), "tensor").sum(0)
        lower = jnp.linalg.cholesky(both[:, tokens:])
        inverse = jax.scipy.linalg.solve_triangular(lower, jnp.eye(rank, dtype=jnp.float32), lower=True)
        token_proj = jnp.dot(inverse, both[:, :tokens], precision=highest)
        per_share = share // row_count
        rows = lax.dynamic_slice_in_dim(left, (index % per_share) * row_count, row_count, 1)
        rows = lax.dynamic_index_in_dim(spread(rows, "tensor"), index // per_share, 0, False)
        basis_mine = jnp.dot(inverse, rows, precision=highest)
        return token_proj, basis_mine

    left = left_stage()
    weight_sent, upper, under, left = tie((weight, grad_output[:half], grad_output[half:], left))
    own, other = weight, lax.ppermute(weight_sent, "dp", swap)
    low = index % 2 == 0
    columns = 2 * row_count
    piece_rows = half // width
    gathered = jnp.zeros((groups, 2, half, grad_output.shape[1]), jnp.bfloat16)
    returned = jnp.zeros((groups, 2, piece_rows, columns), jnp.bfloat16)

    def reduced(pieces):
        rows = jnp.concatenate(pieces, axis=0)
        mine, rest = (
            lax.dot_general(
                rows, part, (((1,), (1,)), ((), ())), preferred_element_type=jnp.float32
            ).astype(jnp.bfloat16)
            for part in (own, other)
        )
        product = jnp.concatenate(
            [jnp.where(low, mine, rest), jnp.where(low, rest, mine)], axis=1
        )
        product = product.reshape(len(pieces), width, piece_rows, columns).transpose(1, 0, 2, 3)
        parts = lax.all_to_all(product, "tensor", 0, 0, tiled=True)
        return parts.astype(jnp.float32).sum(0).astype(jnp.bfloat16)

    def give_back(returned, total, step):
        for place, sign in enumerate((1, -1)):
            value = total[place]
            if step:
                back = [(i, (i - 2 * sign * step) % count) for i in range(count)]
                value = lax.ppermute(value, "dp", back)
            source = (group + sign * step + groups) % groups
            returned = lax.dynamic_update_slice(returned, value[None, None], (source, place, 0, 0))
        return returned

    pieces = []
    for step in range(groups):
        if step == groups - 1:
            total = reduced(pieces)
            for earlier in range(step):
                returned = give_back(returned, total[2 * earlier : 2 * earlier + 2], earlier)
            total = reduced([upper, under])
            returned = give_back(returned, total, step)
        sources = ((group - step + groups) % groups, (group + step) % groups)
        for place, (piece, source) in enumerate(zip((upper, under), sources)):
            gathered = lax.dynamic_update_slice(gathered, piece[None, None], (source, place, 0, 0))
            pieces.append(piece)
        if step + 1 < groups:
            if step == 1:
                upper, under, token_proj = tie((upper, under, token_proj))
            if step == groups - 2:
                upper, under, own, other = tie((upper, under, own, other))
            upper = lax.ppermute(upper, "dp", ahead)
            under = lax.ppermute(under, "dp", behind)
        if step == 0:
            token_proj, basis_mine = basis_stage(left)
    token_proj = spread(token_proj, "dp", along)

    rank = start_basis.shape[1]
    right_part = thin_product(
        token_proj.transpose(1, 0, 2).reshape(rank, groups * tokens),
        gathered.reshape(groups * tokens, -1),
        0,
    ).astype(jnp.bfloat16)
    right_other = lax.ppermute(right_part, "dp", swap)
    right = right_part.astype(jnp.float32) + right_other.astype(jnp.float32)
    right_basis = (right / jnp.sqrt(jnp.float32(tokens * count))).T

    moved = returned
    moved = moved.reshape(groups, 2 * (half // width), columns).transpose(1, 0, 2)
    moved = moved.reshape(2, half // width, width, share).transpose(2, 0, 1, 3)
    moved = lax.all_to_all(moved, "tensor", 0, 0, tiled=True)
    input_grad = moved.transpose(1, 0, 2, 3).reshape(tokens, share)

    basis_upper, basis_lower = split_parts(basis_mine)
    update = lax.dot_general(
        jnp.concatenate([basis_upper, basis_upper, basis_lower, basis_lower], axis=0),
        jnp.concatenate([right_part, right_other, right_part, right_other], axis=0),
        (((0,), (0,)), ((), ())),
        preferred_element_type=jnp.float32,
    )
    new_weight = weight.astype(jnp.float32) - learn_rate * update
    return (input_grad, right_basis, new_weight)


def solution(mesh):
    return jax.shard_map(
        body,
        mesh=mesh,
        in_specs=(P("dp", None), P("dp", "tensor"), P("dp", "tensor"), P("tensor", None)),
        out_specs=(P("dp", "tensor"), P("tensor", None), P("dp", "tensor")),
        check_vma=False,
    )
```
